256 devices in a mesh: design: 16 (over z_hi, y, core), offset: 16 (over z_lo, x).
Axes of the slice: x: 4, y: 4, z: 8 (z_hi: 2, z_lo: 4; z = z_hi * 4 + z_lo), core: 2. Of those that a mesh axis runs over, the one named last changes fastest.
Arguments:
- snapshots: bfloat16 [4096, 256, 1024], P('design', 'offset'), may hold values from -6 to 6
- start_basis: bfloat16 [256, 64, 1024], P('offset'), may hold values from -0.01171875 to 0.01171875
- start_moments: float32 [64, 64], replicated, may hold values from -6 to 6
- station_power: int32 [64], replicated, may hold values from 0 to 4
- girth_power: int32 [64], replicated, may hold values from 0 to 4
- slab_id: int32 [4096], P('design'), may hold values from 0 to 7
- slab_scale: float32 [8], replicated, may hold values from 0.5 to 2
Outputs:
- basis: bfloat16 [256, 64, 1024], P('offset')
- basis_moments: float32 [64, 64], replicated
- moments: float32 [4096, 64], P('design')
The draws below stay inside these ranges and needn't reach their ends.
All inputs are finite; a program needn't handle non-finite values.
Results may differ from the reference program's by a relative error of at most 0.012.
Values may be sent and summed in bfloat16 or wider, within the bound.
A program may use at most 64 MiB of HBM per device.

```python
import math
import jax
import jax.numpy as jnp
from jax import lax

STATIONS = 256
GIRTH = 1024
MOMENTS = 64
K = 64
SLABS = 8
DESIGNS = 4096


def place_ends(entries, own_key, least, largest):
    extent = entries.shape
    index_at = [jax.random.randint(jax.random.fold_in(own_key, axis), (), 0, extent[axis]) for axis in range(len(extent))]
    entries = entries.at[tuple(index_at)].set(least)
    longest = extent.index(max(extent))
    index_at[longest] = (index_at[longest] + 1) % extent[longest]
    return entries.at[tuple(index_at)].set(largest)


def level_of(stream_key, shape, split, low, top_value):
    loudness = 1.0
    for axis_at, blocks in split:
        draws = jax.random.uniform(jax.random.fold_in(jax.random.fold_in(stream_key, 6), axis_at), (blocks,), jnp.float32, low / len(split), top_value / len(split))
        loudness = loudness * jnp.repeat(jnp.exp(draws), shape[axis_at] // blocks).reshape((-1,) + (1,) * (len(shape) - 1 - axis_at))
    return loudness


def noise(stream_key, dims, deviation, bound, split=(), kind=jnp.bfloat16):
    loudness = level_of(stream_key, dims, split, -0.22, 0.18) if split else 1.0
    values = jax.random.normal(stream_key, dims, jnp.float32) * deviation * loudness
    return jnp.minimum(jnp.maximum(values, -bound), bound).astype(kind)


def setup_inputs(seed: int = 0) -> dict:
    key_of = jax.random.split(jax.random.key(seed), 8)
    return {
        "snapshots": noise(key_of[0], (DESIGNS, STATIONS, GIRTH), 1.0, 6.0, ((0, 16), (1, 16))),
        "start_basis": noise(key_of[1], (STATIONS, K, GIRTH), (STATIONS * GIRTH) ** -0.5, 0.01171875, ((0, 16),)),
        "start_moments": noise(key_of[2], (MOMENTS, K), 1.0, 6.0, (), jnp.float32),
        "station_power": place_ends(jax.random.randint(key_of[3], (MOMENTS,), 0, 5), jax.random.fold_in(key_of[3], 1), 0, 4).astype(jnp.int32),
        "girth_power": place_ends(jax.random.randint(key_of[4], (MOMENTS,), 0, 5), jax.random.fold_in(key_of[4], 1), 0, 4).astype(jnp.int32),
        "slab_id": place_ends(jax.random.randint(key_of[5], (DESIGNS,), 0, SLABS), jax.random.fold_in(key_of[5], 1), 0, SLABS - 1).astype(jnp.int32),
        "slab_scale": jnp.clip(jnp.exp(jax.random.uniform(key_of[6], (SLABS,), jnp.float32, math.log(0.5), math.log(2.0))), 0.5, 2.0),
    }


HIGH = lax.Precision.HIGHEST

def power_table(coord, powers):
    table = jnp.stack([coord ** j for j in range(5)], 0)
    picks = (powers[None, :] == jnp.arange(5, dtype=jnp.int32)[:, None]).astype(jnp.float32)
    return jnp.einsum('jp,jm->pm', table, picks, precision=HIGH)

def reference(snapshots, start_basis, start_moments, station_power, girth_power, slab_id, slab_scale):
    t_coord = (jnp.arange(STATIONS, dtype=jnp.float32) + 0.5) / STATIONS
    u_coord = 2.0 * (jnp.arange(GIRTH, dtype=jnp.float32) + 0.5) / GIRTH - 1.0
    station_weight = power_table(t_coord, station_power)
    girth_weight = power_table(u_coord, girth_power).astype(jnp.bfloat16).astype(jnp.float32)
    block = math.gcd(DESIGNS, 256)
    blocks = snapshots.reshape(DESIGNS // block, block, STATIONS, GIRTH)
    basis_full = start_basis.astype(jnp.float32)

    def first(piece):
        whole = piece.astype(jnp.float32)
        inner = jnp.einsum('dsg,gm->dsm', whole, girth_weight, precision=HIGH)
        raw = lax.optimization_barrier(jnp.sum(inner * station_weight[None], 1))
        proj = jnp.einsum('dsg,skg->dk', whole, basis_full, precision=HIGH)
        return (raw, proj)
    raw, proj = lax.map(first, blocks)
    raw = raw.reshape(DESIGNS, MOMENTS)
    proj = proj.reshape(DESIGNS, K)
    picks = (slab_id[:, None] == jnp.arange(SLABS, dtype=jnp.int32)[None, :]).astype(jnp.float32)
    scale = lax.optimization_barrier(jnp.sum(picks * slab_scale[None, :], 1)) / jnp.sqrt(jnp.float32(STATIONS * GIRTH))
    moments = raw * scale[:, None]
    coords = proj + jnp.dot(moments, start_moments, precision=HIGH)
    coords_low = coords.astype(jnp.bfloat16).astype(jnp.float32).reshape(DESIGNS // block, block, K)

    def accumulate(total, pair):
        piece, weights = pair
        return (total + jnp.einsum('dk,dsg->skg', weights, piece.astype(jnp.float32), precision=HIGH), None)
    images, unused = lax.scan(accumulate, jnp.zeros((STATIONS, K, GIRTH), jnp.float32), (blocks, coords_low))
    images_moments = jnp.dot(moments.T, coords_low.reshape(DESIGNS, K), precision=HIGH)
    gram = (jnp.einsum('skg,slg->kl', images, images, precision=HIGH) + jnp.dot(images_moments.T, images_moments, precision=HIGH)) / (STATIONS * GIRTH)
    lower = jnp.linalg.cholesky(gram)
    inverse = lax.linalg.triangular_solve(lower, jnp.eye(K, dtype=jnp.float32), left_side=True, lower=True)
    basis = jnp.einsum('kl,slg->skg', inverse, images, precision=HIGH).astype(jnp.bfloat16)
    basis_moments = jnp.dot(images_moments, inverse.T, precision=HIGH)
    return (basis, basis_moments, moments)
```

```python
import jax
import jax.numpy as jnp
from jax import lax
from jax.experimental import pallas as pl
from jax.experimental.pallas import tpu as pltpu
from jax.sharding import PartitionSpec as P

STATIONS = 256
GIRTH = 1024
SLABS = 8
K = 64
ROWS = 16
DESIGNS = 256
PARTS = 4
WIDE = GIRTH // PARTS

HIGH = lax.Precision.HIGHEST
MESH = pl.DeviceIdType.MESH
F32 = jnp.float32
LOW = jnp.bfloat16


def iota(shape, axis):
    return lax.broadcasted_iota(jnp.int32, shape, axis)


def column(row, lanes):
    n = row.shape[1]
    tall = jnp.where(iota((8, n), 0) == 0, jnp.broadcast_to(row, (8, n)), 0.0)
    return lax.dot_general(
        tall, jnp.ones((8, lanes), F32), (((0,), (0,)), ((), ())),
        precision=HIGH, preferred_element_type=F32,
    )


def power_of(value, powers):
    square = value * value
    out = jnp.where(powers == 0, 1.0, jnp.where(powers == 1, value, square))
    out = jnp.where(powers == 3, square * value, out)
    return jnp.where(powers == 4, square * square, out)


def inverse_factor(matrix):
    eye = (iota((K, K), 0) == iota((K, K), 1)).astype(F32)
    both = jnp.concatenate([matrix, eye], axis=1)
    blocks = [both[8 * b : 8 * b + 8] for b in range(K // 8)]
    sub = iota((8, 1), 0)
    for j in range(K):
        b, r = j // 8, j % 8
        row = blocks[b][r : r + 1, :]
        row = row / row[:, j : j + 1]
        for i in range(b, K // 8):
            col = blocks[i][:, j : j + 1]
            if i == b:
                if r == 7:
                    continue
                col = jnp.where(sub > r, col, 0.0)
            blocks[i] = blocks[i] - col * row
    out = []
    for b in range(K // 8):
        diag = jnp.sum(
            jnp.where(iota((8, 2 * K), 1) == iota((8, 2 * K), 0) + 8 * b, blocks[b], 0.0),
            axis=1, keepdims=True,
        )
        out.append(blocks[b][:, K:] * lax.rsqrt(diag))
    return jnp.concatenate(out, axis=0)


def fold(square):
    return jnp.concatenate([square[: K // 2], square[K // 2 :]], axis=1)


def unfold(folded):
    return jnp.concatenate([folded[:, :K], folded[:, K:]], axis=0)


def kernel(
    snap_hbm, start_hbm, moments_ref, spow_ref, gpow_ref, slab_ref, slab_scale,
    basis_hbm, basis_moments_ref, moments_out,
    raw, turned, weights, acc, scale_ref, parts_ref, coords_ref, girth_ref,
    core_out, core_in, mine, y_out, y_in, z_out, z_in, full, result,
    im_core, im_y, im_z, gram_1, gram_2, gram_3, gram_total,
    load_sem, part_s, part_r, coord_s, coord_r, core_s, core_r, y_s, y_r, z_s, z_r,
    g_s, g_r, f_s, f_r, im_s, im_r, gr_s, gr_r, out_sem,
):
    de, of = lax.axis_index("design"), lax.axis_index("offset")
    c, y, zh = lax.rem(de, 2), lax.rem(de // 2, 4), de // 8
    zl, x = of // 4, lax.rem(of, 4)

    def at(zh_, y_, c_):
        return ((zh_ * 4 + y_) * 2 + c_, of)

    sibling = at(zh, y, 1 - c)
    beyond = at(1 - zh, y, c)

    def along_y(r):
        return at(zh, lax.rem(y + r, 4), c)

    def copy(src, dst, s_sem, r_sem, to):
        return pltpu.make_async_remote_copy(
            src_ref=src, dst_ref=dst, send_sem=s_sem, recv_sem=r_sem,
            device_id=to, device_id_type=MESH,
        )

    barrier = pltpu.get_barrier_semaphore()

    @pl.loop(1, 16)
    def _(r):
        pl.semaphore_signal(barrier, inc=1, device_id=(lax.rem(de + r, 16), of), device_id_type=MESH)
        pl.semaphore_signal(barrier, inc=1, device_id=(de, lax.rem(of + r, 16)), device_id_type=MESH)

    loads = []
    for q in range(PARTS):
        lanes = pl.ds(q * WIDE, WIDE)
        loads.append(pltpu.make_async_copy(snap_hbm.at[:, :, lanes], raw.at[q], load_sem.at[q]))
        loads[-1].start()
        if q == 0:
            start_load = pltpu.make_async_copy(
                start_hbm, weights.at[:, pl.ds(0, K), :], load_sem.at[PARTS]
            )
            start_load.start()

    spow = spow_ref[...]
    gpow = gpow_ref[...]
    u = (2.0 * (iota((K, GIRTH), 1).astype(F32) + 0.5)) / GIRTH - 1.0
    girth_ref[...] = power_of(u, column(gpow.astype(F32), GIRTH).astype(jnp.int32)).astype(LOW)

    @pl.loop(0, ROWS)
    def _(s):
        weights[s, pl.ds(K, K), :] = girth_ref[...]

    slab = slab_ref[...]
    scale = jnp.zeros((1, DESIGNS), F32)
    square = jnp.float32(0.0)
    for j in range(SLABS):
        scale = jnp.where(slab == j, slab_scale[j], scale)
        square = square + slab_scale[j] * slab_scale[j]
    scale = column(scale / 512.0, 2 * K)
    scale_ref[...] = jnp.where(iota((DESIGNS, 2 * K), 1) < K, 1.0, scale)

    lane_power = jnp.concatenate([jnp.zeros((1, K), jnp.int32), spow], axis=1)
    acc[...] = jnp.zeros_like(acc)
    for q in range(PARTS):
        loads[q].wait()

        @pl.loop(0, DESIGNS // 16)
        def _(i):
            d0 = pl.multiple_of(i * 16, 16)
            for g in range(WIDE // 128):
                v = raw[q, pl.ds(d0, 16), :, pl.ds(g * 128, 128)]
                turned[:, pl.ds(d0, 16), pl.ds(q * WIDE + g * 128, 128)] = jnp.swapaxes(v, 0, 1)

        if q == 0:
            start_load.wait()

        @pl.loop(0, ROWS // 4)
        def _(i):
            total = acc[...]
            for j in range(4):
                s = i * 4 + j
                t = ((of * ROWS + s).astype(F32) + 0.5) / STATIONS
                lanes = pl.ds(q * WIDE, WIDE)
                part = lax.dot_general(
                    turned[s, :, lanes], weights[s, :, lanes], (((1,), (1,)), ((), ())),
                    preferred_element_type=F32,
                )
                total = total + part * power_of(t, lane_power)
            acc[...] = total

    pl.semaphore_wait(barrier, 30)

    def row_block(of_):
        return pl.ds(pl.multiple_of(of_ * ROWS, ROWS), ROWS)

    def part_copy(r):
        to = lax.rem(of + r, 16)
        return copy(acc.at[row_block(to)], parts_ref.at[of], part_s.at[r], part_r.at[of], (de, to))

    def part_arrival(r):
        frm = lax.rem(of + r, 16)
        return copy(acc.at[row_block(of)], parts_ref.at[frm], part_s.at[r], part_r.at[frm], (de, frm))

    @pl.loop(1, 16)
    def _(r):
        part_copy(r).start()

    parts_ref[of] = acc[row_block(of), :]

    pc = column(spow.astype(F32), K) + spow.astype(F32)
    qc = column(gpow.astype(F32), K) + gpow.astype(F32)
    even = lax.rem(qc.astype(jnp.int32), 2) == 0
    overlap = jnp.where(even, (square / SLABS) / ((pc + 1.0) * (qc + 1.0)), 0.0)
    start_moments = moments_ref[...]
    model = lax.dot_general(
        start_moments, jnp.dot(overlap, start_moments, precision=HIGH, preferred_element_type=F32),
        (((0,), (0,)), ((), ())), precision=HIGH, preferred_element_type=F32,
    )
    eye = iota((K, K), 0) == iota((K, K), 1)
    model = model + jnp.where(eye, 1.0, 0.0)
    turn = inverse_factor(model)

    @pl.loop(1, 16)
    def _(r):
        part_arrival(r).wait_recv()

    summed = parts_ref[0]
    for j in range(1, 16):
        summed = summed + parts_ref[j]
    summed = summed * scale_ref[row_block(of), :]
    own_moments = summed[:, K:]
    coords = summed[:, :K] + jnp.dot(
        own_moments, start_moments, precision=HIGH, preferred_element_type=F32
    )
    coords = coords.astype(LOW).astype(F32)
    coords = lax.dot_general(
        coords, turn, (((1,), (1,)), ((), ())), precision=HIGH, preferred_element_type=F32
    )
    coords_ref[row_block(of), :] = jnp.concatenate([coords, own_moments], axis=1)

    def coord_copy(r):
        to = lax.rem(of + r, 16)
        return copy(
            coords_ref.at[row_block(of)], coords_ref.at[row_block(of)],
            coord_s.at[r], coord_r.at[of], (de, to),
        )

    def coord_arrival(r):
        frm = lax.rem(of + r, 16)
        return copy(
            coords_ref.at[row_block(frm)], coords_ref.at[row_block(frm)],
            coord_s.at[r], coord_r.at[frm], (de, frm),
        )

    @pl.loop(1, 16)
    def _(r):
        coord_copy(r).start()

    @pl.loop(1, 16)
    def _(r):
        coord_arrival(r).wait_recv()

    coords = coords_ref[:, :K]
    moments = coords_ref[:, K:]
    moments_out[...] = moments
    tall = jnp.transpose(coords_ref[...])[:K].astype(LOW)

    pending = []

    def send(src, dst, s_sem, r_sem, to):
        cp = copy(src, dst, s_sem, r_sem, to)
        cp.start()
        pending.append(cp)
        return cp

    images_moments = lax.dot_general(
        moments, coords, (((0,), (0,)), ((), ())), precision=HIGH, preferred_element_type=F32
    )
    im_core[0] = fold(images_moments)

    def images(q):
        lanes = pl.ds(q * WIDE, WIDE)

        @pl.loop(0, 2)
        def _(i):
            for j in range(4):
                n = i * 4 + j
                core_out[q, n] = jnp.dot(
                    tall, turned[(1 - c) * 8 + n, :, lanes], preferred_element_type=F32
                ).astype(LOW)

        cp = send(core_out.at[q], core_in.at[q], core_s.at[q], core_r.at[q], sibling)

        @pl.loop(0, 2)
        def _(i):
            for j in range(4):
                n = i * 4 + j
                mine[q, n] = jnp.dot(
                    tall, turned[c * 8 + n, :, lanes], preferred_element_type=F32
                )

        return cp

    def to_y(q, cp):
        cp.wait_recv()

        @pl.loop(0, 8)
        def _(n):
            y_out[q, n] = (mine[q, n] + core_in[q, n].astype(F32)).astype(LOW)

        cps = []
        for r in (2, 1, 3):
            pair = pl.ds(2 * lax.rem(y + r, 4), 2)
            cps.append(
                send(y_out.at[q, pair], y_in.at[q, r - 1], y_s.at[q, r - 1], y_r.at[q, r - 1], along_y(r))
            )
        return cps

    def to_z(q, cps):
        for cp in cps:
            cp.wait_recv()
        for h in range(2):
            n = 2 * y + h
            total = mine[q, n] + core_in[q, n].astype(F32)
            for r in range(3):
                total = total + y_in[q, r, h].astype(F32)
            z_out[q, h] = total.astype(LOW)
        return send(z_out.at[q], z_in.at[q], z_s.at[q], z_r.at[q], beyond)

    first = c * 8 + 2 * y

    def gather(q, cp, gram):
        cp.wait_recv()
        for h in range(2):
            image = (z_out[q, h].astype(F32) + z_in[q, h].astype(F32)).astype(LOW)
            full[q, first + h] = image
            gram = gram + lax.dot_general(
                image, image, (((1,), (1,)), ((), ())), preferred_element_type=F32
            )
        pair = full.at[q, pl.ds(first, 2)]
        cps = [
            send(pair, pair, g_s.at[q, r - 1], g_r.at[q, r - 1], along_y(r)) for r in (2, 1, 3)
        ]
        cps.append(send(pair, pair, f_s.at[q, 0], f_r.at[q, 0], sibling))
        return cps, gram

    def hand_on(q, cps):
        for cp, r in zip(cps[:3], (2, 1, 3)):
            cp.wait_recv()
            frm = lax.rem(y + 4 - r, 4)
            pair = full.at[q, pl.ds(c * 8 + 2 * frm, 2)]
            send(pair, pair, f_s.at[q, r], f_r.at[q, r], sibling)

    def exchange(ref, slot, members, sems):
        cps = []
        for r, to in members:
            cps.append(send(ref.at[slot], ref.at[slot], gr_s.at[sems + r], gr_r.at[sems + r], to))
        return cps

    core_im = send(im_core.at[0], im_core.at[1], im_s.at[0], im_r.at[0], sibling)
    core_cp = [None] * PARTS
    y_cp = [None] * PARTS
    z_cp = [None] * PARTS
    g_cp = [None] * PARTS
    core_cp[0] = images(0)
    core_cp[1] = images(1)
    y_cp[0] = to_y(0, core_cp[0])
    core_cp[2] = images(2)
    y_cp[1] = to_y(1, core_cp[1])
    core_im.wait_recv()
    im_y[y] = im_core[0] + im_core[1]
    im_cps = [
        send(im_y.at[y], im_y.at[y], im_s.at[r], im_r.at[r], along_y(r)) for r in (1, 2, 3)
    ]
    core_cp[3] = images(3)
    y_cp[2] = to_y(2, core_cp[2])
    y_cp[3] = to_y(3, core_cp[3])
    for cp in im_cps:
        cp.wait_recv()
    im_z[0] = (im_y[0] + im_y[1]) + (im_y[2] + im_y[3])
    im_cp = send(im_z.at[0], im_z.at[1], im_s.at[4], im_r.at[4], beyond)

    gram = jnp.zeros((K, K), F32)
    z_cp[0] = to_z(0, y_cp[0])
    z_cp[1] = to_z(1, y_cp[1])
    g_cp[0], gram = gather(0, z_cp[0], gram)
    z_cp[2] = to_z(2, y_cp[2])
    g_cp[1], gram = gather(1, z_cp[1], gram)
    z_cp[3] = to_z(3, y_cp[3])
    g_cp[2], gram = gather(2, z_cp[2], gram)
    g_cp[3], gram = gather(3, z_cp[3], gram)

    me = 2 * y + c
    gram_1[me] = fold(gram)
    cps = []
    for r in range(1, 8):
        ry, rc = r // 2, r % 2
        to = at(zh, lax.rem(y + ry, 4), lax.rem(c + rc, 2))
        cps.append((r, to))
    cps = exchange(gram_1, me, cps, 0)
    im_cp.wait_recv()
    images_moments = unfold(im_z[0] + im_z[1])
    hand_on(0, g_cp[0])
    for cp in cps:
        cp.wait_recv()
    total = gram_1[0]
    for j in range(1, 8):
        total = total + gram_1[j]
    gram_2[x] = total
    cps = exchange(gram_2, x, [(r, (de, zl * 4 + lax.rem(x + r, 4))) for r in (1, 2, 3)], 7)
    for cp in cps:
        cp.wait_recv()
    gram_3[zl] = (gram_2[0] + gram_2[1]) + (gram_2[2] + gram_2[3])
    cps = exchange(gram_3, zl, [(r, (de, lax.rem(zl + r, 4) * 4 + x)) for r in (1, 2, 3)], 10)
    hand_on(1, g_cp[1])
    for cp in cps:
        cp.wait_recv()
    gram = unfold((gram_3[0] + gram_3[1]) + (gram_3[2] + gram_3[3]))
    gram = gram + lax.dot_general(
        images_moments, images_moments, (((0,), (0,)), ((), ())),
        precision=HIGH, preferred_element_type=F32,
    )
    inverse = inverse_factor(gram / (STATIONS * GIRTH))
    hand_on(2, g_cp[2])
    hand_on(3, g_cp[3])
    basis_moments_ref[...] = lax.dot_general(
        images_moments, inverse, (((1,), (1,)), ((), ())),
        precision=HIGH, preferred_element_type=F32,
    )
    high = inverse.astype(LOW)
    pieces = jnp.concatenate([high, (inverse - high.astype(F32)).astype(LOW)], axis=0)

    for q in range(PARTS):
        for r in range(4):
            frm = lax.rem(y + 4 - r, 4)
            pair = full.at[q, pl.ds((1 - c) * 8 + 2 * frm, 2)]
            copy(pair, pair, f_s.at[q, r], f_r.at[q, r], sibling).wait_recv()

    outs = []
    for i in range(4):
        for j in range(4):
            s = i * 4 + j
            for q in range(PARTS):
                out = jnp.dot(pieces, full[q, s], preferred_element_type=F32)
                result[s, :, pl.ds(q * WIDE, WIDE)] = (out[:K] + out[K:]).astype(LOW)
        block = pl.ds(i * 4, 4)
        outs.append(pltpu.make_async_copy(result.at[block], basis_hbm.at[block], out_sem.at[i]))
        outs[-1].start()

    @pl.loop(1, 16)
    def _(r):
        part_copy(r).wait_send()
        coord_copy(r).wait_send()

    for cp in pending:
        cp.wait_send()
    for cp in outs:
        cp.wait()


def body(snapshots, start_basis, start_moments, station_power, girth_power, slab_id, slab_scale):
    dma = pltpu.SemaphoreType.DMA
    any_spec = pl.BlockSpec(memory_space=pl.ANY)
    vmem = pl.BlockSpec(memory_space=pltpu.VMEM)
    low = lambda *shape: pltpu.VMEM(shape, LOW)
    wide = lambda *shape: pltpu.VMEM(shape, F32)
    return pl.pallas_call(
        kernel,
        out_shape=(
            jax.ShapeDtypeStruct((ROWS, K, GIRTH), LOW),
            jax.ShapeDtypeStruct((K, K), F32),
            jax.ShapeDtypeStruct((DESIGNS, K), F32),
        ),
        in_specs=[any_spec, any_spec, vmem, vmem, vmem, vmem, pl.BlockSpec(memory_space=pltpu.SMEM)],
        out_specs=(any_spec, vmem, vmem),
        scratch_shapes=[
            low(PARTS, DESIGNS, ROWS, WIDE),
            low(ROWS, DESIGNS, GIRTH),
            low(ROWS, 2 * K, GIRTH),
            wide(DESIGNS, 2 * K),
            wide(DESIGNS, 2 * K),
            wide(16, ROWS, 2 * K),
            wide(DESIGNS, 2 * K),
            low(K, GIRTH),
            low(PARTS, 8, K, WIDE),
            low(PARTS, 8, K, WIDE),
            wide(PARTS, 8, K, WIDE),
            low(PARTS, 8, K, WIDE),
            low(PARTS, 3, 2, K, WIDE),
            low(PARTS, 2, K, WIDE),
            low(PARTS, 2, K, WIDE),
            low(PARTS, ROWS, K, WIDE),
            low(ROWS, K, GIRTH),
            wide(2, K // 2, 2 * K),
            wide(4, K // 2, 2 * K),
            wide(2, K // 2, 2 * K),
            wide(8, K // 2, 2 * K),
            wide(4, K // 2, 2 * K),
            wide(4, K // 2, 2 * K),
            wide(K, K),
            dma((PARTS + 1,)),
            dma((16,)), dma((16,)),
            dma((16,)), dma((16,)),
            dma((PARTS,)), dma((PARTS,)),
            dma((PARTS, 3)), dma((PARTS, 3)),
            dma((PARTS,)), dma((PARTS,)),
            dma((PARTS, 3)), dma((PARTS, 3)),
            dma((PARTS, 4)), dma((PARTS, 4)),
            dma((5,)), dma((5,)),
            dma((14,)), dma((14,)),
            dma((4,)),
        ],
        compiler_params=pltpu.CompilerParams(
            collective_id=0, has_side_effects=True, vmem_limit_bytes=60 << 20
        ),
    )(
        snapshots, start_basis, start_moments,
        station_power.reshape(1, K), girth_power.reshape(1, K),
        slab_id.reshape(1, DESIGNS), slab_scale,
    )


def solution(mesh):
    in_specs = (
        P("design", "offset", None),
        P("offset", None, None),
        P(),
        P(),
        P(),
        P("design"),
        P(),
    )
    out_specs = (P("offset", None, None), P(), P("design", None))
    return jax.shard_map(body, mesh=mesh, in_specs=in_specs, out_specs=out_specs, check_vma=False)
```

```python
import jax
import jax.numpy as jnp
from jax import lax
from jax.experimental import pallas as pl
from jax.experimental.pallas import tpu as pltpu
from jax.sharding import PartitionSpec as P

STATIONS = 256
GIRTH = 1024
SLABS = 8
K = 64
ROWS = 16
DESIGNS = 256
PARTS = 4
WIDE = GIRTH // PARTS

HIGH = lax.Precision.HIGHEST
MESH = pl.DeviceIdType.MESH
F32 = jnp.float32
LOW = jnp.bfloat16


def iota(shape, axis):
    return lax.broadcasted_iota(jnp.int32, shape, axis)


def column(row, lanes):
    n = row.shape[1]
    tall = jnp.where(iota((8, n), 0) == 0, jnp.broadcast_to(row, (8, n)), 0.0)
    return lax.dot_general(
        tall, jnp.ones((8, lanes), F32), (((0,), (0,)), ((), ())),
        precision=HIGH, preferred_element_type=F32,
    )


def power_of(value, powers):
    square = value * value
    out = jnp.where(powers == 0, 1.0, jnp.where(powers == 1, value, square))
    out = jnp.where(powers == 3, square * value, out)
    return jnp.where(powers == 4, square * square, out)


def inverse_factor(matrix, hooks=()):
    eye = (iota((K, K), 0) == iota((K, K), 1)).astype(F32)
    both = jnp.concatenate([matrix, eye], axis=1)
    blocks = [both[8 * b : 8 * b + 8] for b in range(K // 8)]
    sub = iota((8, 1), 0)
    hooks = dict(hooks)
    for j in range(K):
        if j in hooks:
            hooks[j]()
        b, r = j // 8, j % 8
        row = blocks[b][r : r + 1, :]
        row = row / row[:, j : j + 1]
        for i in range(b, K // 8):
            col = blocks[i][:, j : j + 1]
            if i == b:
                if r == 7:
                    continue
                col = jnp.where(sub > r, col, 0.0)
            blocks[i] = blocks[i] - col * row
    out = []
    for b in range(K // 8):
        diag = jnp.sum(
            jnp.where(iota((8, 2 * K), 1) == iota((8, 2 * K), 0) + 8 * b, blocks[b], 0.0),
            axis=1, keepdims=True,
        )
        out.append(blocks[b][:, K:] * lax.rsqrt(diag))
    return jnp.concatenate(out, axis=0)


def fold(square):
    return jnp.concatenate([square[: K // 2], square[K // 2 :]], axis=1)


def unfold(folded):
    return jnp.concatenate([folded[:, :K], folded[:, K:]], axis=0)


def kernel(
    snap_hbm, start_hbm, moments_ref, spow_ref, gpow_ref, slab_ref, slab_scale,
    full, inverse_out, basis_moments_out, moments_out,
    raw, turned_0, turned_1, turned_2, turned_3, weights, acc, scale_ref, parts_ref, coords_ref, girth_ref,
    core_out, core_in, mine, y_out, y_in, z_out, z_in, image_ref,
    im_core, im_y, im_z, gram_1, gram_2, gram_3,
    load_sem, part_s, part_r, coord_s, coord_r, core_s, core_r, y_s, y_r, z_s, z_r,
    g_s, g_r, f_s, f_r, im_s, im_r, gr_s, gr_r, own_sem,
):
    turned = (turned_0, turned_1, turned_2, turned_3)
    de, of = lax.axis_index("design"), lax.axis_index("offset")
    c, y, zh = lax.rem(de, 2), lax.rem(de // 2, 4), de // 8
    zl, x = of // 4, lax.rem(of, 4)

    def at(zh_, y_, c_):
        return ((zh_ * 4 + y_) * 2 + c_, of)

    sibling = at(zh, y, 1 - c)
    beyond = at(1 - zh, y, c)

    def along_y(r):
        return at(zh, lax.rem(y + r, 4), c)

    def copy(src, dst, s_sem, r_sem, to):
        return pltpu.make_async_remote_copy(
            src_ref=src, dst_ref=dst, send_sem=s_sem, recv_sem=r_sem,
            device_id=to, device_id_type=MESH,
        )

    barrier = pltpu.get_barrier_semaphore()

    @pl.loop(1, 16)
    def _(r):
        pl.semaphore_signal(barrier, inc=1, device_id=(lax.rem(de + r, 16), of), device_id_type=MESH)
        pl.semaphore_signal(barrier, inc=1, device_id=(de, lax.rem(of + r, 16)), device_id_type=MESH)

    loads = []
    for q in range(PARTS):
        lanes = pl.ds(q * WIDE, WIDE)
        loads.append(pltpu.make_async_copy(snap_hbm.at[:, :, lanes], raw.at[q], load_sem.at[q]))
        loads[-1].start()
        if q == 0:
            start_load = pltpu.make_async_copy(
                start_hbm, weights.at[:, pl.ds(0, K), :], load_sem.at[PARTS]
            )
            start_load.start()

    spow = spow_ref[...]
    gpow = gpow_ref[...]
    u = (2.0 * (iota((K, GIRTH), 1).astype(F32) + 0.5)) / GIRTH - 1.0
    girth_ref[...] = power_of(u, column(gpow.astype(F32), GIRTH).astype(jnp.int32)).astype(LOW)

    @pl.loop(0, ROWS)
    def _(s):
        weights[s, pl.ds(K, K), :] = girth_ref[...]

    slab = slab_ref[...]
    scale = jnp.zeros((1, DESIGNS), F32)
    square = jnp.float32(0.0)
    for j in range(SLABS):
        scale = jnp.where(slab == j, slab_scale[j], scale)
        square = square + slab_scale[j] * slab_scale[j]
    scale = column(scale / 512.0, 2 * K)
    scale_ref[...] = jnp.where(iota((DESIGNS, 2 * K), 1) < K, 1.0, scale)

    pc = column(spow.astype(F32), K) + spow.astype(F32)
    qc = column(gpow.astype(F32), K) + gpow.astype(F32)
    even = lax.rem(qc.astype(jnp.int32), 2) == 0
    overlap = jnp.where(even, (square / SLABS) / ((pc + 1.0) * (qc + 1.0)), 0.0)
    start_moments = moments_ref[...]
    model = lax.dot_general(
        start_moments, jnp.dot(overlap, start_moments, precision=HIGH, preferred_element_type=F32),
        (((0,), (0,)), ((), ())), precision=HIGH, preferred_element_type=F32,
    )
    eye = iota((K, K), 0) == iota((K, K), 1)
    model = model + jnp.where(eye, 1.0, 0.0)

    lane_power = jnp.concatenate([jnp.zeros((1, K), jnp.int32), spow], axis=1)
    acc[...] = jnp.zeros_like(acc)

    def stand(q, i):
        d0 = pl.multiple_of(i * 16, 16)
        for g in range(WIDE // 128):
            lanes = pl.ds(g * 128, 128)
            turned[q][:, pl.ds(d0, 16), lanes] = jnp.swapaxes(raw[q, pl.ds(d0, 16), :, lanes], 0, 1)

    loads[0].wait()

    for i in range(16):
        stand(0, i)

    start_load.wait()
    for q in range(PARTS):
        if q + 1 < PARTS:
            loads[q + 1].wait()

        total = acc[...]
        for s in range(ROWS):
            t = ((of * ROWS + s).astype(F32) + 0.5) / STATIONS
            part = lax.dot_general(
                turned[q][s], weights[s, :, pl.ds(q * WIDE, WIDE)], (((1,), (1,)), ((), ())),
                preferred_element_type=F32,
            )
            total = total + part * power_of(t, lane_power)
            if q + 1 < PARTS:
                stand(q + 1, s)
        acc[...] = total

    pl.semaphore_wait(barrier, 30)

    def row_block(of_):
        return pl.ds(pl.multiple_of(of_ * ROWS, ROWS), ROWS)

    def part_copy(r):
        to = lax.rem(of + r, 16)
        return copy(acc.at[row_block(to)], parts_ref.at[of], part_s.at[r], part_r.at[of], (de, to))

    def part_arrival(r):
        frm = lax.rem(of + r, 16)
        return copy(acc.at[row_block(of)], parts_ref.at[frm], part_s.at[r], part_r.at[frm], (de, frm))

    @pl.loop(1, 16)
    def _(r):
        part_copy(r).start()

    parts_ref[of] = acc[row_block(of), :]

    turn = inverse_factor(model)

    @pl.loop(1, 16)
    def _(r):
        part_arrival(r).wait_recv()

    summed = parts_ref[0]
    for j in range(1, 16):
        summed = summed + parts_ref[j]
    summed = summed * scale_ref[row_block(of), :]
    own_moments = summed[:, K:]
    coords = summed[:, :K] + jnp.dot(
        own_moments, start_moments, precision=HIGH, preferred_element_type=F32
    )
    coords = coords.astype(LOW).astype(F32)
    coords = lax.dot_general(
        coords, turn, (((1,), (1,)), ((), ())), precision=HIGH, preferred_element_type=F32
    )
    coords_ref[row_block(of), :] = jnp.concatenate([coords, own_moments], axis=1)

    def coord_copy(r):
        to = lax.rem(of + r, 16)
        return copy(
            coords_ref.at[row_block(of)], coords_ref.at[row_block(of)],
            coord_s.at[r], coord_r.at[of], (de, to),
        )

    def coord_arrival(r):
        frm = lax.rem(of + r, 16)
        return copy(
            coords_ref.at[row_block(frm)], coords_ref.at[row_block(frm)],
            coord_s.at[r], coord_r.at[frm], (de, frm),
        )

    @pl.loop(1, 16)
    def _(r):
        coord_copy(r).start()

    @pl.loop(1, 16)
    def _(r):
        coord_arrival(r).wait_recv()

    coords = coords_ref[:, :K]
    moments = coords_ref[:, K:]
    upright = jnp.transpose(coords_ref[...])
    moments_out[...] = upright[K:]
    tall = upright[:K].astype(LOW)

    pending = []

    def send(src, dst, s_sem, r_sem, to):
        cp = copy(src, dst, s_sem, r_sem, to)
        cp.start()
        pending.append(cp)
        return cp

    images_moments = lax.dot_general(
        moments, coords, (((0,), (0,)), ((), ())), precision=HIGH, preferred_element_type=F32
    )
    im_core[0] = fold(images_moments)

    def images(q):
        for n in range(8):
            core_out[q, n] = jnp.dot(
                tall, turned[q][(1 - c) * 8 + n], preferred_element_type=F32
            ).astype(LOW)

        cp = send(core_out.at[q], core_in.at[q], core_s.at[q], core_r.at[q], sibling)

        for n in range(8):
            mine[q, n] = jnp.dot(tall, turned[q][c * 8 + n], preferred_element_type=F32)

        return cp

    def to_y(q, cp):
        cp.wait_recv()

        for n in range(8):
            y_out[q, n] = (mine[q, n] + core_in[q, n].astype(F32)).astype(LOW)

        cps = []
        for r in (2, 1, 3):
            pair = pl.ds(2 * lax.rem(y + r, 4), 2)
            cps.append(
                send(y_out.at[q, pair], y_in.at[q, r - 1], y_s.at[q, r - 1], y_r.at[q, r - 1], along_y(r))
            )
        return cps

    def to_z(q, cps):
        for cp in cps:
            cp.wait_recv()
        for h in range(2):
            n = 2 * y + h
            total = mine[q, n] + core_in[q, n].astype(F32)
            for r in range(3):
                total = total + y_in[q, r, h].astype(F32)
            z_out[q, h] = total.astype(LOW)
        return send(z_out.at[q], z_in.at[q], z_s.at[q], z_r.at[q], beyond)

    first = c * 8 + 2 * y

    def settle(q, cp, gram):
        cp.wait_recv()
        for h in range(2):
            image = (z_out[q, h].astype(F32) + z_in[q, h].astype(F32)).astype(LOW)
            image_ref[q, h] = image
            gram = gram + lax.dot_general(
                image, image, (((1,), (1,)), ((), ())), preferred_element_type=F32
            )
        return gram

    own = []

    def gather(q):
        pair = full.at[q, pl.ds(first, 2)]
        cps = [
            send(image_ref.at[q], pair, g_s.at[q, r - 1], g_r.at[q, r - 1], along_y(r))
            for r in (2, 1, 3)
        ]
        send(image_ref.at[q], pair, f_s.at[q, 0], f_r.at[q, 0], sibling)
        own.append(pltpu.make_async_copy(image_ref.at[q], pair, own_sem.at[q]))
        own[-1].start()
        return cps

    def hand_on(q):
        for cp, r in zip(g_cp[q], (2, 1, 3)):
            cp.wait_recv()
            frm = lax.rem(y + 4 - r, 4)
            pair = full.at[q, pl.ds(c * 8 + 2 * frm, 2)]
            send(pair, pair, f_s.at[q, r], f_r.at[q, r], sibling)

    def exchange(ref, slot, members, sems):
        cps = []
        for r, to in members:
            cps.append(send(ref.at[slot], ref.at[slot], gr_s.at[sems + r], gr_r.at[sems + r], to))
        return cps

    core_cp = [None] * PARTS
    y_cp = [None] * PARTS
    z_cp = [None] * PARTS
    g_cp = [None] * PARTS
    core_cp[0] = images(0)
    core_im = send(im_core.at[0], im_core.at[1], im_s.at[0], im_r.at[0], sibling)
    core_cp[1] = images(1)
    y_cp[0] = to_y(0, core_cp[0])
    core_cp[2] = images(2)
    y_cp[1] = to_y(1, core_cp[1])
    core_cp[3] = images(3)
    core_im.wait_recv()
    im_y[y] = im_core[0] + im_core[1]
    im_cps = [
        send(im_y.at[y], im_y.at[y], im_s.at[r], im_r.at[r], along_y(r)) for r in (1, 2, 3)
    ]
    z_cp[0] = to_z(0, y_cp[0])
    y_cp[2] = to_y(2, core_cp[2])
    for cp in im_cps:
        cp.wait_recv()
    im_z[0] = (im_y[0] + im_y[1]) + (im_y[2] + im_y[3])
    im_cp = send(im_z.at[0], im_z.at[1], im_s.at[4], im_r.at[4], beyond)
    z_cp[1] = to_z(1, y_cp[1])
    y_cp[3] = to_y(3, core_cp[3])
    z_cp[2] = to_z(2, y_cp[2])
    z_cp[3] = to_z(3, y_cp[3])

    gram = jnp.zeros((K, K), F32)
    gram = settle(0, z_cp[0], gram)
    g_cp[0] = gather(0)
    gram = settle(1, z_cp[1], gram)
    g_cp[1] = gather(1)
    im_cp.wait_recv()
    images_moments = unfold(im_z[0] + im_z[1])
    moments_part = lax.dot_general(
        images_moments, images_moments, (((0,), (0,)), ((), ())),
        precision=HIGH, preferred_element_type=F32,
    )
    gram = settle(2, z_cp[2], gram)
    gram = settle(3, z_cp[3], gram)

    me = 2 * y + c
    gram_1[me] = fold(gram)
    cps = []
    for r in range(1, 8):
        to = at(zh, lax.rem(y + r // 2, 4), lax.rem(c + r % 2, 2))
        cps.append((r, to))
    cps = exchange(gram_1, me, cps, 0)
    g_cp[2] = gather(2)
    g_cp[3] = gather(3)
    for cp in cps:
        cp.wait_recv()
    total = gram_1[0]
    for j in range(1, 8):
        total = total + gram_1[j]
    gram_2[x] = total
    cps = exchange(gram_2, x, [(r, (de, zl * 4 + lax.rem(x + r, 4))) for r in (2, 1, 3)], 7)
    hand_on(0)
    for cp in cps:
        cp.wait_recv()
    gram_3[zl] = (gram_2[0] + gram_2[1]) + (gram_2[2] + gram_2[3])
    cps = exchange(gram_3, zl, [(r, (de, lax.rem(zl + r, 4) * 4 + x)) for r in (2, 1, 3)], 10)
    hand_on(1)
    for cp in cps:
        cp.wait_recv()
    gram = unfold((gram_3[0] + gram_3[1]) + (gram_3[2] + gram_3[3])) + moments_part
    inverse = inverse_factor(
        gram / (STATIONS * GIRTH), [(24, lambda: hand_on(2)), (48, lambda: hand_on(3))]
    )
    basis_moments_out[...] = lax.dot_general(
        images_moments, inverse, (((1,), (1,)), ((), ())),
        precision=HIGH, preferred_element_type=F32,
    )
    high = inverse.astype(LOW)
    inverse_out[...] = jnp.concatenate([high, (inverse - high.astype(F32)).astype(LOW)], axis=0)

    for q in range(PARTS):
        for r in range(4):
            frm = lax.rem(y + 4 - r, 4)
            pair = full.at[q, pl.ds((1 - c) * 8 + 2 * frm, 2)]
            copy(pair, pair, f_s.at[q, r], f_r.at[q, r], sibling).wait_recv()

    @pl.loop(1, 16)
    def _(r):
        part_copy(r).wait_send()
        coord_copy(r).wait_send()

    for cp in pending:
        cp.wait_send()
    for cp in own:
        cp.wait()


def finish(
    full, pieces_ref, basis_moments_in, moments_in, basis_hbm, basis_moments_ref, moments_ref,
    images, result, in_sem, out_sem, small_sem,
):
    loads = [
        pltpu.make_async_copy(full.at[q], images.at[q], in_sem.at[q]) for q in range(PARTS)
    ]
    for cp in loads:
        cp.start()
    outs = [
        pltpu.make_async_copy(basis_moments_in, basis_moments_ref, small_sem.at[0]),
        pltpu.make_async_copy(moments_in, moments_ref, small_sem.at[1]),
    ]
    for cp in outs:
        cp.start()
    pieces = pieces_ref[...]
    for q in range(PARTS):
        loads[q].wait()

        for s in range(ROWS):
            out = jnp.dot(pieces, images[q, s], preferred_element_type=F32)
            result[q, s] = (out[:K] + out[K:]).astype(LOW)

        outs.append(
            pltpu.make_async_copy(
                result.at[q], basis_hbm.at[:, :, pl.ds(q * WIDE, WIDE)], out_sem.at[q]
            )
        )
        outs[-1].start()
    for cp in outs:
        cp.wait()


def body(snapshots, start_basis, start_moments, station_power, girth_power, slab_id, slab_scale):
    dma = pltpu.SemaphoreType.DMA
    any_spec = pl.BlockSpec(memory_space=pl.ANY)
    vmem = pl.BlockSpec(memory_space=pltpu.VMEM)
    low = lambda *shape: pltpu.VMEM(shape, LOW)
    wide = lambda *shape: pltpu.VMEM(shape, F32)
    full, pieces, basis_moments, moments = pl.pallas_call(
        kernel,
        out_shape=(
            jax.ShapeDtypeStruct((PARTS, ROWS, K, WIDE), LOW),
            jax.ShapeDtypeStruct((2 * K, K), LOW),
            jax.ShapeDtypeStruct((K, K), F32),
            jax.ShapeDtypeStruct((K, DESIGNS), F32),
        ),
        in_specs=[any_spec, any_spec, vmem, vmem, vmem, vmem, pl.BlockSpec(memory_space=pltpu.SMEM)],
        out_specs=(any_spec, vmem, vmem, vmem),
        scratch_shapes=[
            low(PARTS, DESIGNS, ROWS, WIDE),
            *[low(ROWS, DESIGNS, WIDE)] * PARTS,
            low(ROWS, 2 * K, GIRTH),
            wide(DESIGNS, 2 * K),
            wide(DESIGNS, 2 * K),
            wide(16, ROWS, 2 * K),
            wide(DESIGNS, 2 * K),
            low(K, GIRTH),
            low(PARTS, 8, K, WIDE),
            low(PARTS, 8, K, WIDE),
            wide(PARTS, 8, K, WIDE),
            low(PARTS, 8, K, WIDE),
            low(PARTS, 3, 2, K, WIDE),
            low(PARTS, 2, K, WIDE),
            low(PARTS, 2, K, WIDE),
            low(PARTS, 2, K, WIDE),
            wide(2, K // 2, 2 * K),
            wide(4, K // 2, 2 * K),
            wide(2, K // 2, 2 * K),
            wide(8, K // 2, 2 * K),
            wide(4, K // 2, 2 * K),
            wide(4, K // 2, 2 * K),
            dma((PARTS + 1,)),
            dma((16,)), dma((16,)),
            dma((16,)), dma((16,)),
            dma((PARTS,)), dma((PARTS,)),
            dma((PARTS, 3)), dma((PARTS, 3)),
            dma((PARTS,)), dma((PARTS,)),
            dma((PARTS, 3)), dma((PARTS, 3)),
            dma((PARTS, 4)), dma((PARTS, 4)),
            dma((5,)), dma((5,)),
            dma((14,)), dma((14,)),
            dma((4,)),
        ],
        compiler_params=pltpu.CompilerParams(
            collective_id=0, has_side_effects=True, vmem_limit_bytes=60 << 20
        ),
    )(
        snapshots, start_basis, start_moments,
        station_power.reshape(1, K), girth_power.reshape(1, K),
        slab_id.reshape(1, DESIGNS), slab_scale,
    )
    basis, basis_moments, moments = pl.pallas_call(
        finish,
        out_shape=(
            jax.ShapeDtypeStruct((ROWS, K, GIRTH), LOW),
            jax.ShapeDtypeStruct((K, K), F32),
            jax.ShapeDtypeStruct((K, DESIGNS), F32),
        ),
        in_specs=[any_spec, vmem, any_spec, any_spec],
        out_specs=(any_spec, any_spec, any_spec),
        scratch_shapes=[
            low(PARTS, ROWS, K, WIDE),
            low(PARTS, ROWS, K, WIDE),
            dma((PARTS,)), dma((PARTS,)), dma((2,)),
        ],
        compiler_params=pltpu.CompilerParams(vmem_limit_bytes=60 << 20),
    )(full, pieces, basis_moments, moments)
    return basis, basis_moments, moments.T


def solution(mesh):
    in_specs = (
        P("design", "offset", None),
        P("offset", None, None),
        P(),
        P(),
        P(),
        P("design"),
        P(),
    )
    out_specs = (P("offset", None, None), P(), P("design", None))
    return jax.shard_map(body, mesh=mesh, in_specs=in_specs, out_specs=out_specs, check_vma=False)
```

```python
import jax
import jax.numpy as jnp
from jax import lax
from jax.experimental import pallas as pl
from jax.experimental.pallas import tpu as pltpu
from jax.sharding import PartitionSpec as P

STATIONS = 256
GIRTH = 1024
SLABS = 8
K = 64
ROWS = 16
DESIGNS = 256
PARTS = 4
WIDE = GIRTH // PARTS
TRAVEL = 8
NARROW = GIRTH // TRAVEL

HIGH = lax.Precision.HIGHEST
MESH = pl.DeviceIdType.MESH
F32 = jnp.float32
LOW = jnp.bfloat16


def iota(shape, axis):
    return lax.broadcasted_iota(jnp.int32, shape, axis)


def column(row, lanes):
    n = row.shape[1]
    tall = jnp.where(iota((8, n), 0) == 0, jnp.broadcast_to(row, (8, n)), 0.0)
    return lax.dot_general(
        tall, jnp.ones((8, lanes), F32), (((0,), (0,)), ((), ())),
        precision=HIGH, preferred_element_type=F32,
    )


def power_of(value, powers):
    square = value * value
    out = jnp.where(powers == 0, 1.0, jnp.where(powers == 1, value, square))
    out = jnp.where(powers == 3, square * value, out)
    return jnp.where(powers == 4, square * square, out)


def inverse_factor(matrix, hooks=()):
    eye = (iota((K, K), 0) == iota((K, K), 1)).astype(F32)
    both = jnp.concatenate([matrix, eye], axis=1)
    blocks = [both[8 * b : 8 * b + 8] for b in range(K // 8)]
    sub = iota((8, 1), 0)
    hooks = dict(hooks)
    for j in range(K):
        if j in hooks:
            hooks[j]()
        b, r = j // 8, j % 8
        row = blocks[b][r : r + 1, :]
        row = row / row[:, j : j + 1]
        for i in range(b, K // 8):
            col = blocks[i][:, j : j + 1]
            if i == b:
                if r == 7:
                    continue
                col = jnp.where(sub > r, col, 0.0)
            blocks[i] = blocks[i] - col * row
    out = []
    for b in range(K // 8):
        diag = jnp.sum(
            jnp.where(iota((8, 2 * K), 1) == iota((8, 2 * K), 0) + 8 * b, blocks[b], 0.0),
            axis=1, keepdims=True,
        )
        out.append(blocks[b][:, K:] * lax.rsqrt(diag))
    return jnp.concatenate(out, axis=0)


def fold(square):
    return jnp.concatenate([square[: K // 2], square[K // 2 :]], axis=1)


def unfold(folded):
    return jnp.concatenate([folded[:, :K], folded[:, K:]], axis=0)


def kernel(
    snap_hbm, start_hbm, moments_hbm, spow_hbm, gpow_hbm, slab_hbm, slab_scale_hbm,
    full, inverse_out, basis_moments_out, moments_out,
    moments_ref, spow_ref, gpow_ref, slab_ref, slab_scale_ref,
    raw, turned_0, turned_1, turned_2, turned_3, weights, acc, scale_ref, parts_ref, coords_ref, girth_ref,
    core_out, core_in, mine, y_out, y_in, z_out, z_in, image_ref,
    im_core, im_y, im_z, gram_1, gram_2, gram_3,
    load_sem, part_s, part_r, coord_s, coord_r, core_s, core_r, y_s, y_r, z_s, z_r,
    g_s, g_r, f_s, f_r, im_s, im_r, gr_s, gr_r, own_sem, small_sem,
):
    turned = (turned_0, turned_1, turned_2, turned_3)
    de, of = lax.axis_index("design"), lax.axis_index("offset")
    c, y, zh = lax.rem(de, 2), lax.rem(de // 2, 4), de // 8
    zl, x = of // 4, lax.rem(of, 4)

    def at(zh_, y_, c_):
        return ((zh_ * 4 + y_) * 2 + c_, of)

    sibling = at(zh, y, 1 - c)
    beyond = at(1 - zh, y, c)

    def along_y(r):
        return at(zh, lax.rem(y + r, 4), c)

    def copy(src, dst, s_sem, r_sem, to):
        return pltpu.make_async_remote_copy(
            src_ref=src, dst_ref=dst, send_sem=s_sem, recv_sem=r_sem,
            device_id=to, device_id_type=MESH,
        )

    small = [
        pltpu.make_async_copy(src, dst, small_sem.at[i])
        for i, (src, dst) in enumerate(
            (
                (spow_hbm, spow_ref), (gpow_hbm, gpow_ref), (moments_hbm, moments_ref),
                (slab_hbm, slab_ref), (slab_scale_hbm, slab_scale_ref),
            )
        )
    ]
    for cp in small:
        cp.start()
    loads = []
    for q in range(PARTS):
        lanes = pl.ds(q * WIDE, WIDE)
        loads.append(pltpu.make_async_copy(snap_hbm.at[:, :, lanes], raw.at[q], load_sem.at[q]))
        if q < 2:
            loads[-1].start()
        if q == 0:
            start_load = pltpu.make_async_copy(
                start_hbm, weights.at[:, pl.ds(0, K), :], load_sem.at[PARTS]
            )
            start_load.start()

    barrier = pltpu.get_barrier_semaphore()

    @pl.loop(1, 16)
    def _(r):
        pl.semaphore_signal(barrier, inc=1, device_id=(lax.rem(de + r, 16), of), device_id_type=MESH)
        pl.semaphore_signal(barrier, inc=1, device_id=(de, lax.rem(of + r, 16)), device_id_type=MESH)

    def along_z(r):
        z = lax.rem(zh * 4 + zl + r + 8, 8)
        return ((z // 4) * 8 + lax.rem(de, 8), lax.rem(z, 4) * 4 + x)

    for r in (1, -1, 2, -2):
        pl.semaphore_signal(barrier, inc=1, device_id=along_z(r), device_id_type=MESH)

    for cp in small:
        cp.wait()

    spow = spow_ref[...]
    gpow = gpow_ref[...]
    u = (2.0 * (iota((K, GIRTH), 1).astype(F32) + 0.5)) / GIRTH - 1.0
    girth_ref[...] = power_of(u, column(gpow.astype(F32), GIRTH).astype(jnp.int32)).astype(LOW)

    @pl.loop(0, ROWS)
    def _(s):
        weights[s, pl.ds(K, K), :] = girth_ref[...]

    slab = slab_ref[...]
    slab_scale = slab_scale_ref[...]
    scale = jnp.zeros((1, DESIGNS), F32)
    square = jnp.sum(slab_scale * slab_scale, axis=1, keepdims=True)
    for j in range(SLABS):
        scale = jnp.where(slab == j, slab_scale[:, j : j + 1], scale)
    scale = column(scale / 512.0, 2 * K)
    scale_ref[...] = jnp.where(iota((DESIGNS, 2 * K), 1) < K, 1.0, scale)

    pc = column(spow.astype(F32), K) + spow.astype(F32)
    qc = column(gpow.astype(F32), K) + gpow.astype(F32)
    even = lax.rem(qc.astype(jnp.int32), 2) == 0
    overlap = jnp.where(even, (square / SLABS) / ((pc + 1.0) * (qc + 1.0)), 0.0)
    start_moments = moments_ref[...]
    model = lax.dot_general(
        start_moments, jnp.dot(overlap, start_moments, precision=HIGH, preferred_element_type=F32),
        (((0,), (0,)), ((), ())), precision=HIGH, preferred_element_type=F32,
    )
    eye = iota((K, K), 0) == iota((K, K), 1)
    model = model + jnp.where(eye, 1.0, 0.0)

    lane_power = jnp.concatenate([jnp.zeros((1, K), jnp.int32), spow], axis=1)
    acc[...] = jnp.zeros_like(acc)

    def stand(q, i):
        d0 = pl.multiple_of(i * 16, 16)
        for g in range(WIDE // 128):
            lanes = pl.ds(g * 128, 128)
            turned[q][:, pl.ds(d0, 16), lanes] = jnp.swapaxes(raw[q, pl.ds(d0, 16), :, lanes], 0, 1)

    def dots(q, total, s):
        t = ((of * ROWS + s).astype(F32) + 0.5) / STATIONS
        part = lax.dot_general(
            jnp.concatenate([turned[q][s], turned[q + 1][s]], axis=1),
            weights[s, :, pl.ds(q * WIDE, 2 * WIDE)], (((1,), (1,)), ((), ())),
            preferred_element_type=F32,
        )
        return total + part * power_of(t, lane_power)

    for q in range(2):
        loads[q].wait()
        if q + 2 < PARTS:
            loads[q + 2].start()
        for i in range(16):
            stand(q, i)
    start_load.wait()
    total = jnp.zeros((DESIGNS, 2 * K), F32)
    for q in range(2, 4):
        loads[q].wait()
        if q + 2 < PARTS:
            loads[q + 2].start()
        for i in range(16):
            stand(q, i)
            if i % 2 == 0:
                total = dots(0, total, (q - 2) * 8 + i // 2)
    for s in range(ROWS):
        total = dots(2, total, s)
    acc[...] = total

    pl.semaphore_wait(barrier, 34)

    def row_block(of_):
        return pl.ds(pl.multiple_of(of_ * ROWS, ROWS), ROWS)

    def part_copy(r):
        to = lax.rem(of + r, 16)
        return copy(acc.at[row_block(to)], parts_ref.at[of], part_s.at[r], part_r.at[of], (de, to))

    def part_arrival(r):
        frm = lax.rem(of + r, 16)
        return copy(acc.at[row_block(of)], parts_ref.at[frm], part_s.at[r], part_r.at[frm], (de, frm))

    @pl.loop(1, 16)
    def _(r):
        part_copy(r).start()

    parts_ref[of] = acc[row_block(of), :]

    turn = inverse_factor(model)

    @pl.loop(1, 16)
    def _(r):
        part_arrival(r).wait_recv()

    summed = parts_ref[0]
    for j in range(1, 16):
        summed = summed + parts_ref[j]
    summed = summed * scale_ref[row_block(of), :]
    own_moments = summed[:, K:]
    coords = summed[:, :K] + jnp.dot(
        own_moments, start_moments, precision=HIGH, preferred_element_type=F32
    )
    coords = coords.astype(LOW).astype(F32)
    coords = lax.dot_general(
        coords, turn, (((1,), (1,)), ((), ())), precision=HIGH, preferred_element_type=F32
    )
    coords_ref[row_block(of), :] = jnp.concatenate([coords, own_moments], axis=1)

    def coord_copy(r):
        to = lax.rem(of + r, 16)
        return copy(
            coords_ref.at[row_block(of)], coords_ref.at[row_block(of)],
            coord_s.at[r], coord_r.at[of], (de, to),
        )

    def coord_arrival(r):
        frm = lax.rem(of + r, 16)
        return copy(
            coords_ref.at[row_block(frm)], coords_ref.at[row_block(frm)],
            coord_s.at[r], coord_r.at[frm], (de, frm),
        )

    @pl.loop(1, 16)
    def _(r):
        coord_copy(r).start()

    @pl.loop(1, 16)
    def _(r):
        coord_arrival(r).wait_recv()

    coords = coords_ref[:, :K]
    moments = coords_ref[:, K:]
    upright = jnp.transpose(coords_ref[...])
    moments_out[...] = upright[K:]
    tall = upright[:K].astype(LOW)

    pending = []

    def send(src, dst, s_sem, r_sem, to):
        cp = copy(src, dst, s_sem, r_sem, to)
        cp.start()
        pending.append(cp)
        return cp

    def images(q):
        for n in range(8):
            core_out[q, n] = jnp.dot(
                tall, turned[q][(1 - c) * 8 + n], preferred_element_type=F32
            ).astype(LOW)

        cp = send(core_out.at[q], core_in.at[q], core_s.at[q], core_r.at[q], sibling)

        for n in range(8):
            mine[q, n] = jnp.dot(tall, turned[q][c * 8 + n], preferred_element_type=F32)

        return cp

    def place(p):
        return p * NARROW // WIDE, pl.ds(p * NARROW % WIDE, NARROW)

    def to_y(p):
        q, lanes = place(p)
        if p * NARROW % WIDE == 0:
            core_cp[q].wait_recv()
        for n in range(8):
            y_out[p, n] = (mine[q, n, :, lanes] + core_in[q, n, :, lanes].astype(F32)).astype(LOW)
        cps = []
        for r in (2, 1, 3):
            pair = pl.ds(2 * lax.rem(y + r, 4), 2)
            cps.append(
                send(y_out.at[p, pair], y_in.at[p, r - 1], y_s.at[p, r - 1], y_r.at[p, r - 1], along_y(r))
            )
        y_cp[p] = cps

    def to_z(p):
        q, lanes = place(p)
        for cp in y_cp[p]:
            cp.wait_recv()
        for h in range(2):
            n = 2 * y + h
            total = mine[q, n, :, lanes] + core_in[q, n, :, lanes].astype(F32)
            for r in range(3):
                total = total + y_in[p, r, h].astype(F32)
            z_out[p, h] = total.astype(LOW)
        z_cp[p] = send(z_out.at[p], z_in.at[p], z_s.at[p], z_r.at[p], beyond)

    first = c * 8 + 2 * y

    def settle(p, gram):
        q, lanes = place(p)
        z_cp[p].wait_recv()
        for h in range(2):
            image = (z_out[p, h].astype(F32) + z_in[p, h].astype(F32)).astype(LOW)
            image_ref[q, h, :, lanes] = image
            gram = gram + lax.dot_general(
                image, image, (((1,), (1,)), ((), ())), preferred_element_type=F32
            )
        return gram

    own = []

    def gather(q):
        pair = full.at[q, pl.ds(first, 2)]
        cps = [
            send(image_ref.at[q], pair, g_s.at[q, r - 1], g_r.at[q, r - 1], along_y(r))
            for r in (2, 1, 3)
        ]
        send(image_ref.at[q], pair, f_s.at[q, 0], f_r.at[q, 0], sibling)
        own.append(pltpu.make_async_copy(image_ref.at[q], pair, own_sem.at[q]))
        own[-1].start()
        return cps

    def hand_on(q):
        for cp, r in zip(g_cp[q], (2, 1, 3)):
            cp.wait_recv()
            frm = lax.rem(y + 4 - r, 4)
            pair = full.at[q, pl.ds(c * 8 + 2 * frm, 2)]
            send(pair, pair, f_s.at[q, r], f_r.at[q, r], sibling)

    def exchange(ref, slot, members, sems):
        cps = []
        for r, to in members:
            cps.append(send(ref.at[slot], ref.at[slot], gr_s.at[sems + r], gr_r.at[sems + r], to))
        return cps

    core_cp = [None] * PARTS
    y_cp = [None] * TRAVEL
    z_cp = [None] * TRAVEL
    g_cp = [None] * PARTS
    per = TRAVEL // PARTS
    core_cp[0] = images(0)
    core_cp[1] = images(1)
    for p in range(per):
        to_y(p)
    core_cp[2] = images(2)
    for p in range(per, 2 * per):
        to_y(p)
    core_cp[3] = images(3)
    images_moments = lax.dot_general(
        moments, coords, (((0,), (0,)), ((), ())), precision=HIGH, preferred_element_type=F32
    )
    im_core[0] = fold(images_moments)
    core_im = send(im_core.at[0], im_core.at[1], im_s.at[0], im_r.at[0], sibling)
    for p in range(TRAVEL):
        to_z(p)
        if p + 2 * per < TRAVEL:
            to_y(p + 2 * per)
        if p == 0:
            core_im.wait_recv()
            im_y[y] = im_core[0] + im_core[1]
            im_cps = [
                send(im_y.at[y], im_y.at[y], im_s.at[r], im_r.at[r], along_y(r)) for r in (1, 2, 3)
            ]
        if p == TRAVEL - 2:
            for cp in im_cps:
                cp.wait_recv()
            im_z[0] = (im_y[0] + im_y[1]) + (im_y[2] + im_y[3])
            im_cp = send(im_z.at[0], im_z.at[1], im_s.at[4], im_r.at[4], beyond)

    gram = jnp.zeros((K, K), F32)
    for p in range(per):
        gram = settle(p, gram)
    g_cp[0] = gather(0)
    for p in range(per, 2 * per):
        gram = settle(p, gram)
    g_cp[1] = gather(1)
    im_cp.wait_recv()
    images_moments = unfold(im_z[0] + im_z[1])
    moments_part = lax.dot_general(
        images_moments, images_moments, (((0,), (0,)), ((), ())),
        precision=HIGH, preferred_element_type=F32,
    )
    for p in range(2 * per, TRAVEL):
        gram = settle(p, gram)

    me = 2 * y + c
    gram_1[me] = fold(gram)
    cps = []
    for r in range(1, 8):
        to = at(zh, lax.rem(y + r // 2, 4), lax.rem(c + r % 2, 2))
        cps.append((r, to))
    cps = exchange(gram_1, me, cps, 0)
    g_cp[2] = gather(2)
    g_cp[3] = gather(3)
    for cp in cps:
        cp.wait_recv()
    total = gram_1[0]
    for j in range(1, 8):
        total = total + gram_1[j]
    gram_2[x] = total
    cps = exchange(gram_2, x, [(r, (de, zl * 4 + lax.rem(x + r, 4))) for r in (2, 1, 3)], 7)
    hand_on(0)
    for cp in cps:
        cp.wait_recv()
    gram_3[zl] = (gram_2[0] + gram_2[1]) + (gram_2[2] + gram_2[3])
    cps = exchange(gram_3, zl, [(r, along_z(d)) for r, d in ((2, 2), (1, 1), (3, -1))], 10)
    hand_on(1)
    for cp in cps:
        cp.wait_recv()
    gram = unfold((gram_3[0] + gram_3[1]) + (gram_3[2] + gram_3[3])) + moments_part
    inverse = inverse_factor(
        gram / (STATIONS * GIRTH), [(24, lambda: hand_on(2)), (48, lambda: hand_on(3))]
    )
    basis_moments_out[...] = lax.dot_general(
        images_moments, inverse, (((1,), (1,)), ((), ())),
        precision=HIGH, preferred_element_type=F32,
    )
    high = inverse.astype(LOW)
    inverse_out[...] = jnp.concatenate([high, (inverse - high.astype(F32)).astype(LOW)], axis=0)

    for q in range(PARTS):
        for r in range(4):
            frm = lax.rem(y + 4 - r, 4)
            pair = full.at[q, pl.ds((1 - c) * 8 + 2 * frm, 2)]
            copy(pair, pair, f_s.at[q, r], f_r.at[q, r], sibling).wait_recv()

    @pl.loop(1, 16)
    def _(r):
        part_copy(r).wait_send()
        coord_copy(r).wait_send()

    for cp in pending:
        cp.wait_send()
    for cp in own:
        cp.wait()


def finish(
    full, pieces_hbm, basis_moments_in, moments_in, basis_hbm, basis_moments_ref, moments_ref,
    images, result, pieces_ref, in_sem, out_sem, small_sem,
):
    loads = [
        pltpu.make_async_copy(full.at[q], images.at[q], in_sem.at[q]) for q in range(PARTS)
    ]
    get = pltpu.make_async_copy(pieces_hbm, pieces_ref, small_sem.at[2])
    get.start()
    for cp in loads:
        cp.start()
    outs = [
        pltpu.make_async_copy(basis_moments_in, basis_moments_ref, small_sem.at[0]),
        pltpu.make_async_copy(moments_in, moments_ref, small_sem.at[1]),
    ]
    for cp in outs:
        cp.start()
    get.wait()
    pieces = pieces_ref[...]
    for q in range(PARTS):
        loads[q].wait()

        for s in range(ROWS):
            out = jnp.dot(pieces, images[q, s], preferred_element_type=F32)
            result[q, s] = (out[:K] + out[K:]).astype(LOW)

        outs.append(
            pltpu.make_async_copy(
                result.at[q], basis_hbm.at[:, :, pl.ds(q * WIDE, WIDE)], out_sem.at[q]
            )
        )
        outs[-1].start()
    for cp in outs:
        cp.wait()


def body(snapshots, start_basis, start_moments, station_power, girth_power, slab_id, slab_scale):
    dma = pltpu.SemaphoreType.DMA
    any_spec = pl.BlockSpec(memory_space=pl.ANY)
    vmem = pl.BlockSpec(memory_space=pltpu.VMEM)
    low = lambda *shape: pltpu.VMEM(shape, LOW)
    wide = lambda *shape: pltpu.VMEM(shape, F32)
    full, pieces, basis_moments, moments = pl.pallas_call(
        kernel,
        out_shape=(
            jax.ShapeDtypeStruct((PARTS, ROWS, K, WIDE), LOW),
            jax.ShapeDtypeStruct((2 * K, K), LOW),
            jax.ShapeDtypeStruct((K, K), F32),
            jax.ShapeDtypeStruct((K, DESIGNS), F32),
        ),
        in_specs=[any_spec] * 7,
        out_specs=(any_spec, vmem, vmem, vmem),
        scratch_shapes=[
            wide(K, K),
            pltpu.VMEM((1, K), jnp.int32),
            pltpu.VMEM((1, K), jnp.int32),
            pltpu.VMEM((1, DESIGNS), jnp.int32),
            wide(1, SLABS),
            low(PARTS, DESIGNS, ROWS, WIDE),
            *[low(ROWS, DESIGNS, WIDE)] * PARTS,
            low(ROWS, 2 * K, GIRTH),
            wide(DESIGNS, 2 * K),
            wide(DESIGNS, 2 * K),
            wide(16, ROWS, 2 * K),
            wide(DESIGNS, 2 * K),
            low(K, GIRTH),
            low(PARTS, 8, K, WIDE),
            low(PARTS, 8, K, WIDE),
            wide(PARTS, 8, K, WIDE),
            low(TRAVEL, 8, K, NARROW),
            low(TRAVEL, 3, 2, K, NARROW),
            low(TRAVEL, 2, K, NARROW),
            low(TRAVEL, 2, K, NARROW),
            low(PARTS, 2, K, WIDE),
            wide(2, K // 2, 2 * K),
            wide(4, K // 2, 2 * K),
            wide(2, K // 2, 2 * K),
            wide(8, K // 2, 2 * K),
            wide(4, K // 2, 2 * K),
            wide(4, K // 2, 2 * K),
            dma((PARTS + 1,)),
            dma((16,)), dma((16,)),
            dma((16,)), dma((16,)),
            dma((PARTS,)), dma((PARTS,)),
            dma((TRAVEL, 3)), dma((TRAVEL, 3)),
            dma((TRAVEL,)), dma((TRAVEL,)),
            dma((PARTS, 3)), dma((PARTS, 3)),
            dma((PARTS, 4)), dma((PARTS, 4)),
            dma((5,)), dma((5,)),
            dma((14,)), dma((14,)),
            dma((4,)),
            dma((5,)),
        ],
        compiler_params=pltpu.CompilerParams(
            collective_id=0, has_side_effects=True, vmem_limit_bytes=60 << 20
        ),
    )(
        snapshots, start_basis, start_moments,
        station_power.reshape(1, K), girth_power.reshape(1, K),
        slab_id.reshape(1, DESIGNS), slab_scale.reshape(1, SLABS),
    )
    basis, basis_moments, moments = pl.pallas_call(
        finish,
        out_shape=(
            jax.ShapeDtypeStruct((ROWS, K, GIRTH), LOW),
            jax.ShapeDtypeStruct((K, K), F32),
            jax.ShapeDtypeStruct((K, DESIGNS), F32),
        ),
        in_specs=[any_spec] * 4,
        out_specs=(any_spec, any_spec, any_spec),
        scratch_shapes=[
            low(PARTS, ROWS, K, WIDE),
            low(PARTS, ROWS, K, WIDE),
            low(2 * K, K),
            dma((PARTS,)), dma((PARTS,)), dma((3,)),
        ],
        compiler_params=pltpu.CompilerParams(vmem_limit_bytes=60 << 20),
    )(full, pieces, basis_moments, moments)
    return basis, basis_moments, moments.T


def solution(mesh):
    in_specs = (
        P("design", "offset", None),
        P("offset", None, None),
        P(),
        P(),
        P(),
        P("design"),
        P(),
    )
    out_specs = (P("offset", None, None), P(), P("design", None))
    return jax.shard_map(body, mesh=mesh, in_specs=in_specs, out_specs=out_specs, check_vma=False)
```

```python
import jax
import jax.numpy as jnp
from jax import lax
from jax.experimental import pallas as pl
from jax.experimental.pallas import tpu as pltpu
from jax.sharding import PartitionSpec as P

STATIONS = 256
GIRTH = 1024
SLABS = 8
K = 64
ROWS = 16
DESIGNS = 256
PARTS = 4
WIDE = GIRTH // PARTS
TRAVEL = 8
NARROW = GIRTH // TRAVEL

HIGH = lax.Precision.HIGHEST
MESH = pl.DeviceIdType.MESH
F32 = jnp.float32
LOW = jnp.bfloat16


def iota(shape, axis):
    return lax.broadcasted_iota(jnp.int32, shape, axis)


def column(row, lanes):
    n = row.shape[1]
    tall = jnp.where(iota((8, n), 0) == 0, jnp.broadcast_to(row, (8, n)), 0.0)
    return lax.dot_general(
        tall, jnp.ones((8, lanes), F32), (((0,), (0,)), ((), ())),
        precision=HIGH, preferred_element_type=F32,
    )


def power_of(value, powers):
    square = value * value
    out = jnp.where(powers == 0, 1.0, jnp.where(powers == 1, value, square))
    out = jnp.where(powers == 3, square * value, out)
    return jnp.where(powers == 4, square * square, out)


def inverse_factor(matrix, hooks=()):
    eye = (iota((K, K), 0) == iota((K, K), 1)).astype(F32)
    both = jnp.concatenate([matrix, eye], axis=1)
    blocks = [both[8 * b : 8 * b + 8] for b in range(K // 8)]
    sub = iota((8, 1), 0)
    hooks = dict(hooks)
    for j in range(K):
        if j in hooks:
            hooks[j]()
        b, r = j // 8, j % 8
        row = blocks[b][r : r + 1, :]
        row = row * (1.0 / row[:, j : j + 1])
        for i in range(b, K // 8):
            col = blocks[i][:, j : j + 1]
            if i == b:
                if r == 7:
                    continue
                col = jnp.where(sub > r, col, 0.0)
            blocks[i] = blocks[i] - col * row
    out = []
    for b in range(K // 8):
        diag = jnp.sum(
            jnp.where(iota((8, 2 * K), 1) == iota((8, 2 * K), 0) + 8 * b, blocks[b], 0.0),
            axis=1, keepdims=True,
        )
        out.append(blocks[b][:, K:] * lax.rsqrt(diag))
    return jnp.concatenate(out, axis=0)


def fold(square):
    return jnp.concatenate([square[: K // 2], square[K // 2 :]], axis=1)


def unfold(folded):
    return jnp.concatenate([folded[:, :K], folded[:, K:]], axis=0)


def kernel(
    snap_hbm, start_hbm, moments_hbm, spow_hbm, gpow_hbm, slab_hbm, slab_scale_hbm,
    full, inverse_out, basis_moments_out, moments_out,
    moments_ref, spow_ref, gpow_ref, slab_ref, slab_scale_ref,
    raw, turned_0, turned_1, turned_2, turned_3, weights, acc, scale_ref, parts_ref, coords_ref, girth_ref,
    core_out, core_in, mine, y_out, y_in, z_out, z_in, image_ref,
    im_core, im_y, im_z, gram_1, gram_2, gram_3,
    load_sem, part_s, part_r, coord_s, coord_r, core_s, core_r, y_s, y_r, z_s, z_r,
    g_s, g_r, f_s, f_r, im_s, im_r, gr_s, gr_r, own_sem, small_sem,
):
    turned = (turned_0, turned_1, turned_2, turned_3)
    de, of = lax.axis_index("design"), lax.axis_index("offset")
    c, y, zh = lax.rem(de, 2), lax.rem(de // 2, 4), de // 8
    zl, x = of // 4, lax.rem(of, 4)

    def at(zh_, y_, c_):
        return ((zh_ * 4 + y_) * 2 + c_, of)

    sibling = at(zh, y, 1 - c)
    beyond = at(1 - zh, y, c)

    def along_y(r):
        return at(zh, lax.rem(y + r, 4), c)

    def copy(src, dst, s_sem, r_sem, to):
        return pltpu.make_async_remote_copy(
            src_ref=src, dst_ref=dst, send_sem=s_sem, recv_sem=r_sem,
            device_id=to, device_id_type=MESH,
        )

    small = [
        pltpu.make_async_copy(src, dst, small_sem.at[i])
        for i, (src, dst) in enumerate(
            (
                (spow_hbm, spow_ref), (gpow_hbm, gpow_ref), (moments_hbm, moments_ref),
                (slab_hbm, slab_ref), (slab_scale_hbm, slab_scale_ref),
            )
        )
    ]
    for cp in small:
        cp.start()
    loads = []
    for q in range(PARTS):
        lanes = pl.ds(q * WIDE, WIDE)
        loads.append(pltpu.make_async_copy(snap_hbm.at[:, :, lanes], raw.at[q], load_sem.at[q]))
        if q < 2:
            loads[-1].start()
        if q == 0:
            start_load = pltpu.make_async_copy(
                start_hbm, weights.at[:, pl.ds(0, K), :], load_sem.at[PARTS]
            )
            start_load.start()

    barrier = pltpu.get_barrier_semaphore()

    @pl.loop(1, 16)
    def _(r):
        pl.semaphore_signal(barrier, inc=1, device_id=(lax.rem(de + r, 16), of), device_id_type=MESH)
        pl.semaphore_signal(barrier, inc=1, device_id=(de, lax.rem(of + r, 16)), device_id_type=MESH)

    def along_z(r):
        z = lax.rem(zh * 4 + zl + r + 8, 8)
        return ((z // 4) * 8 + lax.rem(de, 8), lax.rem(z, 4) * 4 + x)

    for r in (1, -1, 2, -2):
        pl.semaphore_signal(barrier, inc=1, device_id=along_z(r), device_id_type=MESH)

    for cp in small:
        cp.wait()

    spow = spow_ref[...]
    gpow = gpow_ref[...]
    u = (2.0 * (iota((K, GIRTH), 1).astype(F32) + 0.5)) / GIRTH - 1.0
    girth_ref[...] = power_of(u, column(gpow.astype(F32), GIRTH).astype(jnp.int32)).astype(LOW)

    @pl.loop(0, ROWS)
    def _(s):
        weights[s, pl.ds(K, K), :] = girth_ref[...]

    slab = slab_ref[...]
    slab_scale = slab_scale_ref[...]
    scale = jnp.zeros((1, DESIGNS), F32)
    square = jnp.sum(slab_scale * slab_scale, axis=1, keepdims=True)
    for j in range(SLABS):
        scale = jnp.where(slab == j, slab_scale[:, j : j + 1], scale)
    scale = column(scale / 512.0, 2 * K)
    scale_ref[...] = jnp.where(iota((DESIGNS, 2 * K), 1) < K, 1.0, scale)

    pc = column(spow.astype(F32), K) + spow.astype(F32)
    qc = column(gpow.astype(F32), K) + gpow.astype(F32)
    even = lax.rem(qc.astype(jnp.int32), 2) == 0
    overlap = jnp.where(even, (square / SLABS) / ((pc + 1.0) * (qc + 1.0)), 0.0)
    start_moments = moments_ref[...]
    model = lax.dot_general(
        start_moments, jnp.dot(overlap, start_moments, precision=HIGH, preferred_element_type=F32),
        (((0,), (0,)), ((), ())), precision=HIGH, preferred_element_type=F32,
    )
    eye = iota((K, K), 0) == iota((K, K), 1)
    model = model + jnp.where(eye, 1.0, 0.0)

    lane_power = jnp.concatenate([jnp.zeros((1, K), jnp.int32), spow], axis=1)
    acc[...] = jnp.zeros_like(acc)

    def stand(q, i):
        d0 = pl.multiple_of(i * 16, 16)
        for g in range(WIDE // 128):
            lanes = pl.ds(g * 128, 128)
            turned[q][:, pl.ds(d0, 16), lanes] = jnp.swapaxes(raw[q, pl.ds(d0, 16), :, lanes], 0, 1)

    def dots(q, total, s):
        t = ((of * ROWS + s).astype(F32) + 0.5) / STATIONS
        part = lax.dot_general(
            jnp.concatenate([turned[q][s], turned[q + 1][s]], axis=1),
            weights[s, :, pl.ds(q * WIDE, 2 * WIDE)], (((1,), (1,)), ((), ())),
            preferred_element_type=F32,
        )
        return total + part * power_of(t, lane_power)

    for q in range(2):
        loads[q].wait()
        if q + 2 < PARTS:
            loads[q + 2].start()
        for i in range(16):
            stand(q, i)
    start_load.wait()
    total = jnp.zeros((DESIGNS, 2 * K), F32)
    for q in range(2, 4):
        loads[q].wait()
        if q + 2 < PARTS:
            loads[q + 2].start()
        for i in range(16):
            stand(q, i)
            if i % 2 == 0:
                total = dots(0, total, (q - 2) * 8 + i // 2)
    for s in range(ROWS):
        total = dots(2, total, s)
    acc[...] = total

    pl.semaphore_wait(barrier, 34)

    def row_block(of_):
        return pl.ds(pl.multiple_of(of_ * ROWS, ROWS), ROWS)

    def part_copy(r):
        to = lax.rem(of + r, 16)
        return copy(acc.at[row_block(to)], parts_ref.at[of], part_s.at[r], part_r.at[of], (de, to))

    def part_arrival(r):
        frm = lax.rem(of + r, 16)
        return copy(acc.at[row_block(of)], parts_ref.at[frm], part_s.at[r], part_r.at[frm], (de, frm))

    @pl.loop(1, 16)
    def _(r):
        part_copy(r).start()

    parts_ref[of] = acc[row_block(of), :]

    turn = inverse_factor(model)

    @pl.loop(1, 16)
    def _(r):
        part_arrival(r).wait_recv()

    summed = parts_ref[0]
    for j in range(1, 16):
        summed = summed + parts_ref[j]
    summed = summed * scale_ref[row_block(of), :]
    own_moments = summed[:, K:]
    coords = summed[:, :K] + jnp.dot(
        own_moments, start_moments, precision=HIGH, preferred_element_type=F32
    )
    coords = coords.astype(LOW).astype(F32)
    coords = lax.dot_general(
        coords, turn, (((1,), (1,)), ((), ())), precision=HIGH, preferred_element_type=F32
    )
    coords_ref[row_block(of), :] = jnp.concatenate([coords, own_moments], axis=1)

    def coord_copy(r):
        to = lax.rem(of + r, 16)
        return copy(
            coords_ref.at[row_block(of)], coords_ref.at[row_block(of)],
            coord_s.at[r], coord_r.at[of], (de, to),
        )

    def coord_arrival(r):
        frm = lax.rem(of + r, 16)
        return copy(
            coords_ref.at[row_block(frm)], coords_ref.at[row_block(frm)],
            coord_s.at[r], coord_r.at[frm], (de, frm),
        )

    @pl.loop(1, 16)
    def _(r):
        coord_copy(r).start()

    @pl.loop(1, 16)
    def _(r):
        coord_arrival(r).wait_recv()

    coords = coords_ref[:, :K]
    moments = coords_ref[:, K:]
    upright = jnp.transpose(coords_ref[...])
    moments_out[...] = upright[K:]
    tall = upright[:K].astype(LOW)

    pending = []

    def send(src, dst, s_sem, r_sem, to):
        cp = copy(src, dst, s_sem, r_sem, to)
        cp.start()
        pending.append(cp)
        return cp

    def images(q):
        for n in range(8):
            core_out[q, n] = jnp.dot(
                tall, turned[q][(1 - c) * 8 + n], preferred_element_type=F32
            ).astype(LOW)

        cp = send(core_out.at[q], core_in.at[q], core_s.at[q], core_r.at[q], sibling)

        for n in range(8):
            mine[q, n] = jnp.dot(tall, turned[q][c * 8 + n], preferred_element_type=F32)

        return cp

    def place(p):
        return p * NARROW // WIDE, pl.ds(p * NARROW % WIDE, NARROW)

    def to_y(p):
        q, lanes = place(p)
        if p * NARROW % WIDE == 0:
            core_cp[q].wait_recv()
        for n in range(8):
            y_out[p, n] = (mine[q, n, :, lanes] + core_in[q, n, :, lanes].astype(F32)).astype(LOW)
        cps = []
        for r in (2, 1, 3):
            pair = pl.ds(2 * lax.rem(y + r, 4), 2)
            cps.append(
                send(y_out.at[p, pair], y_in.at[p, r - 1], y_s.at[p, r - 1], y_r.at[p, r - 1], along_y(r))
            )
        y_cp[p] = cps

    def to_z(p):
        q, lanes = place(p)
        for cp in y_cp[p]:
            cp.wait_recv()
        for h in range(2):
            n = 2 * y + h
            total = mine[q, n, :, lanes] + core_in[q, n, :, lanes].astype(F32)
            for r in range(3):
                total = total + y_in[p, r, h].astype(F32)
            z_out[p, h] = total.astype(LOW)
        z_cp[p] = send(z_out.at[p], z_in.at[p], z_s.at[p], z_r.at[p], beyond)

    first = c * 8 + 2 * y

    def settle(p, gram):
        q, lanes = place(p)
        z_cp[p].wait_recv()
        for h in range(2):
            image = (z_out[p, h].astype(F32) + z_in[p, h].astype(F32)).astype(LOW)
            image_ref[q, h, :, lanes] = image
            gram = gram + lax.dot_general(
                image, image, (((1,), (1,)), ((), ())), preferred_element_type=F32
            )
        return gram

    own = []

    def gather(q):
        pair = full.at[q, pl.ds(first, 2)]
        cps = [
            send(image_ref.at[q], pair, g_s.at[q, r], g_r.at[q, r], along_y(2 * r + 1))
            for r in range(2)
        ]
        send(image_ref.at[q], pair, f_s.at[q, 0], f_r.at[q, 0], sibling)
        own.append(pltpu.make_async_copy(image_ref.at[q], pair, own_sem.at[q]))
        own[-1].start()
        return cps

    def hand_on(q):
        for cp, r in zip(g_cp[q], range(2)):
            cp.wait_recv()
            frm = lax.rem(y + 3 - 2 * r, 4)
            station = full.at[q, pl.ds(c * 8 + 2 * frm + r, 1)]
            relay[q].append(
                send(station, station, g_s.at[q, 2 + r], g_r.at[q, 2 + r], along_y(2 * r + 1))
            )
            pair = full.at[q, pl.ds(c * 8 + 2 * frm, 2)]
            send(pair, pair, f_s.at[q, 1 + r], f_r.at[q, 1 + r], sibling)

    relay = [[] for q in range(PARTS)]

    def hand_on_far(q):
        for cp in relay[q]:
            cp.wait_recv()
        pair = full.at[q, pl.ds(c * 8 + 2 * lax.rem(y + 2, 4), 2)]
        send(pair, pair, f_s.at[q, 3], f_r.at[q, 3], sibling)

    def exchange(ref, slot, members, sems):
        cps = []
        for r, to in members:
            cps.append(send(ref.at[slot], ref.at[slot], gr_s.at[sems + r], gr_r.at[sems + r], to))
        return cps

    core_cp = [None] * PARTS
    y_cp = [None] * TRAVEL
    z_cp = [None] * TRAVEL
    g_cp = [None] * PARTS
    per = TRAVEL // PARTS
    core_cp[0] = images(0)
    core_cp[1] = images(1)
    for p in range(per):
        to_y(p)
    core_cp[2] = images(2)
    for p in range(per, 2 * per):
        to_y(p)
    core_cp[3] = images(3)
    images_moments = lax.dot_general(
        moments, coords, (((0,), (0,)), ((), ())), precision=HIGH, preferred_element_type=F32
    )
    im_core[0] = fold(images_moments)
    core_im = send(im_core.at[0], im_core.at[1], im_s.at[0], im_r.at[0], sibling)
    for p in range(TRAVEL):
        to_z(p)
        if p + 2 * per < TRAVEL:
            to_y(p + 2 * per)
        if p == 0:
            core_im.wait_recv()
            im_y[y] = im_core[0] + im_core[1]
            im_cps = [
                send(im_y.at[y], im_y.at[y], im_s.at[r], im_r.at[r], along_y(r)) for r in (1, 2, 3)
            ]
        if p == TRAVEL - 2:
            for cp in im_cps:
                cp.wait_recv()
            im_z[0] = (im_y[0] + im_y[1]) + (im_y[2] + im_y[3])
            im_cp = send(im_z.at[0], im_z.at[1], im_s.at[4], im_r.at[4], beyond)

    gram = jnp.zeros((K, K), F32)
    for p in range(per):
        gram = settle(p, gram)
    g_cp[0] = gather(0)
    for p in range(per, 2 * per):
        gram = settle(p, gram)
    im_cp.wait_recv()
    images_moments = unfold(im_z[0] + im_z[1])
    moments_part = lax.dot_general(
        images_moments, images_moments, (((0,), (0,)), ((), ())),
        precision=HIGH, preferred_element_type=F32,
    )
    for p in range(2 * per, TRAVEL):
        gram = settle(p, gram)

    me = 2 * y + c
    gram_1[me] = fold(gram)
    cps = []
    for r in range(1, 8):
        to = at(zh, lax.rem(y + r // 2, 4), lax.rem(c + r % 2, 2))
        cps.append((r, to))
    cps = exchange(gram_1, me, cps, 0)
    g_cp[1] = gather(1)
    g_cp[2] = gather(2)
    g_cp[3] = gather(3)
    for cp in cps:
        cp.wait_recv()
    total = gram_1[0]
    for j in range(1, 8):
        total = total + gram_1[j]
    gram_2[x] = total
    cps = exchange(gram_2, x, [(r, (de, zl * 4 + lax.rem(x + r, 4))) for r in (2, 1, 3)], 7)
    hand_on(0)
    for cp in cps:
        cp.wait_recv()
    gram_3[zl] = (gram_2[0] + gram_2[1]) + (gram_2[2] + gram_2[3])
    cps = exchange(gram_3, zl, [(r, along_z(d)) for r, d in ((2, 2), (1, 1), (3, -1))], 10)
    hand_on(1)
    hand_on_far(0)
    for cp in cps:
        cp.wait_recv()
    gram = unfold((gram_3[0] + gram_3[1]) + (gram_3[2] + gram_3[3])) + moments_part
    inverse = inverse_factor(
        gram / (STATIONS * GIRTH), [(0, lambda: hand_on(2)), (16, lambda: hand_on(3)), (32, lambda: hand_on_far(1)), (40, lambda: hand_on_far(2)), (56, lambda: hand_on_far(3))]
    )
    basis_moments_out[...] = lax.dot_general(
        images_moments, inverse, (((1,), (1,)), ((), ())),
        precision=HIGH, preferred_element_type=F32,
    )
    high = inverse.astype(LOW)
    inverse_out[...] = jnp.concatenate([high, (inverse - high.astype(F32)).astype(LOW)], axis=0)

    for q in range(PARTS):
        for r in range(4):
            frm = lax.rem(y + 4 - r, 4)
            pair = full.at[q, pl.ds((1 - c) * 8 + 2 * frm, 2)]
            copy(pair, pair, f_s.at[q, r], f_r.at[q, r], sibling).wait_recv()

    @pl.loop(1, 16)
    def _(r):
        part_copy(r).wait_send()
        coord_copy(r).wait_send()

    for cp in pending:
        cp.wait_send()
    for cp in own:
        cp.wait()


def finish(
    full, pieces_hbm, basis_moments_in, moments_in, basis_hbm, basis_moments_ref, moments_ref,
    images, result, pieces_ref, in_sem, out_sem, small_sem,
):
    loads = [
        pltpu.make_async_copy(full.at[q], images.at[q], in_sem.at[q]) for q in range(PARTS)
    ]
    get = pltpu.make_async_copy(pieces_hbm, pieces_ref, small_sem.at[2])
    get.start()
    for cp in loads:
        cp.start()
    outs = [
        pltpu.make_async_copy(basis_moments_in, basis_moments_ref, small_sem.at[0]),
        pltpu.make_async_copy(moments_in, moments_ref, small_sem.at[1]),
    ]
    for cp in outs:
        cp.start()
    get.wait()
    pieces = pieces_ref[...]
    for q in range(PARTS):
        loads[q].wait()

        for s in range(ROWS):
            out = jnp.dot(pieces, images[q, s], preferred_element_type=F32)
            result[q, s] = (out[:K] + out[K:]).astype(LOW)

        outs.append(
            pltpu.make_async_copy(
                result.at[q], basis_hbm.at[:, :, pl.ds(q * WIDE, WIDE)], out_sem.at[q]
            )
        )
        outs[-1].start()
    for cp in outs:
        cp.wait()


def body(snapshots, start_basis, start_moments, station_power, girth_power, slab_id, slab_scale):
    dma = pltpu.SemaphoreType.DMA
    any_spec = pl.BlockSpec(memory_space=pl.ANY)
    vmem = pl.BlockSpec(memory_space=pltpu.VMEM)
    low = lambda *shape: pltpu.VMEM(shape, LOW)
    wide = lambda *shape: pltpu.VMEM(shape, F32)
    full, pieces, basis_moments, moments = pl.pallas_call(
        kernel,
        out_shape=(
            jax.ShapeDtypeStruct((PARTS, ROWS, K, WIDE), LOW),
            jax.ShapeDtypeStruct((2 * K, K), LOW),
            jax.ShapeDtypeStruct((K, K), F32),
            jax.ShapeDtypeStruct((K, DESIGNS), F32),
        ),
        in_specs=[any_spec] * 7,
        out_specs=(any_spec, vmem, vmem, vmem),
        scratch_shapes=[
            wide(K, K),
            pltpu.VMEM((1, K), jnp.int32),
            pltpu.VMEM((1, K), jnp.int32),
            pltpu.VMEM((1, DESIGNS), jnp.int32),
            wide(1, SLABS),
            low(PARTS, DESIGNS, ROWS, WIDE),
            *[low(ROWS, DESIGNS, WIDE)] * PARTS,
            low(ROWS, 2 * K, GIRTH),
            wide(DESIGNS, 2 * K),
            wide(DESIGNS, 2 * K),
            wide(16, ROWS, 2 * K),
            wide(DESIGNS, 2 * K),
            low(K, GIRTH),
            low(PARTS, 8, K, WIDE),
            low(PARTS, 8, K, WIDE),
            wide(PARTS, 8, K, WIDE),
            low(TRAVEL, 8, K, NARROW),
            low(TRAVEL, 3, 2, K, NARROW),
            low(TRAVEL, 2, K, NARROW),
            low(TRAVEL, 2, K, NARROW),
            low(PARTS, 2, K, WIDE),
            wide(2, K // 2, 2 * K),
            wide(4, K // 2, 2 * K),
            wide(2, K // 2, 2 * K),
            wide(8, K // 2, 2 * K),
            wide(4, K // 2, 2 * K),
            wide(4, K // 2, 2 * K),
            dma((PARTS + 1,)),
            dma((16,)), dma((16,)),
            dma((16,)), dma((16,)),
            dma((PARTS,)), dma((PARTS,)),
            dma((TRAVEL, 3)), dma((TRAVEL, 3)),
            dma((TRAVEL,)), dma((TRAVEL,)),
            dma((PARTS, 4)), dma((PARTS, 4)),
            dma((PARTS, 4)), dma((PARTS, 4)),
            dma((5,)), dma((5,)),
            dma((14,)), dma((14,)),
            dma((4,)),
            dma((5,)),
        ],
        compiler_params=pltpu.CompilerParams(
            collective_id=0, has_side_effects=True, vmem_limit_bytes=60 << 20
        ),
    )(
        snapshots, start_basis, start_moments,
        station_power.reshape(1, K), girth_power.reshape(1, K),
        slab_id.reshape(1, DESIGNS), slab_scale.reshape(1, SLABS),
    )
    basis, basis_moments, moments = pl.pallas_call(
        finish,
        out_shape=(
            jax.ShapeDtypeStruct((ROWS, K, GIRTH), LOW),
            jax.ShapeDtypeStruct((K, K), F32),
            jax.ShapeDtypeStruct((K, DESIGNS), F32),
        ),
        in_specs=[any_spec] * 4,
        out_specs=(any_spec, any_spec, any_spec),
        scratch_shapes=[
            low(PARTS, ROWS, K, WIDE),
            low(PARTS, ROWS, K, WIDE),
            low(2 * K, K),
            dma((PARTS,)), dma((PARTS,)), dma((3,)),
        ],
        compiler_params=pltpu.CompilerParams(vmem_limit_bytes=60 << 20),
    )(full, pieces, basis_moments, moments)
    return basis, basis_moments, moments.T


def solution(mesh):
    in_specs = (
        P("design", "offset", None),
        P("offset", None, None),
        P(),
        P(),
        P(),
        P("design"),
        P(),
    )
    out_specs = (P("offset", None, None), P(), P("design", None))
    return jax.shard_map(body, mesh=mesh, in_specs=in_specs, out_specs=out_specs, check_vma=False)
```
